1024 devices in a mesh: dp: 16 (over y, core), expert: 64 (over x, z).
Axes of the slice: x: 4, y: 8, z: 16, core: 2. Of those that a mesh axis runs over, the one named last changes fastest.
Arguments:
- tokens: bfloat16 [131072, 512], P(('dp', 'expert')), may hold values from -40 to 40
- norm_gain: float32 [512], replicated, may hold values from 0.5 to 1.5
- routes: int32 [131072, 2], P(('dp', 'expert')), may hold values from 0 to 63, all different within a row; in each aligned block of 128 rows (0 to 127, 128 to 255, ...) at most 5 rows name the same one
- gate_weights: float32 [131072, 2], P(('dp', 'expert')), may hold values from 0.05 to 1
- weight_in: bfloat16 [64, 2048, 512], P('expert'), may hold values from -0.25 to 0.25
- weight_out: bfloat16 [64, 2048, 512], P('expert'), may hold values from -0.125 to 0.125
- out_grad: bfloat16 [131072, 512], P(('dp', 'expert')), may hold values from -1.5 to 1.5
Outputs:
- mixed: bfloat16 [131072, 512], P(('dp', 'expert'))
- gate_grad: float32 [131072, 2], P(('dp', 'expert'))
- token_grad: bfloat16 [131072, 512], P(('dp', 'expert'))
- w_in_grad: float32 [64, 2048, 512], P('expert', 'dp')
- w_out_grad: float32 [64, 2048, 512], P('expert', 'dp')
The draws below stay inside these ranges and needn't reach their ends.
Inputs may be any that keep to these rules, and one draw needn't show every extreme that they name: `routes`: each frame names 2 different experts; among the frames of one device no expert is named more than 5 times.
All inputs are finite; a program needn't handle non-finite values.
Results may differ from the reference program's by a relative error of at most 0.022.
Values may be sent and summed in bfloat16 or wider, within the bound.
A program may use at most 64 MiB of HBM per device.

```python
import math
import jax
import jax.numpy as jnp
import numpy as np
from jax import lax

D = 512
HID = 2048
TOP = 2
TOK_DEV = 128
EXPERTS = 64
CAP = 5
TOKENS = 131072
N_DP = 16


def draw_tokens(key, part):
    keys = jax.random.split(key, 4)
    row_scale = jnp.exp(jax.random.uniform(keys[0], (TOKENS, 1), jnp.float32, math.log(0.3), math.log(3.0)))
    col_scale = jnp.exp(jax.random.uniform(keys[1], (1, D), jnp.float32, math.log(0.3), math.log(3.0)))
    shift_v = jax.random.uniform(keys[2], (TOKENS, 1), jnp.float32, -1.0, 1.0)
    noise_v = jax.random.truncated_normal(keys[3], -4.0, 4.0, (TOKENS, D), jnp.float32)
    return (row_scale * (col_scale * noise_v + shift_v)).astype(jnp.bfloat16)


def levels(stream_key, shape, cuts, low, top_value):
    level, own = 1.0, jax.random.fold_in(stream_key, 6)
    for position, parts in cuts:
        heights = jnp.exp(jax.random.uniform(jax.random.fold_in(own, position), (parts,), jnp.float32, low / len(cuts), top_value / len(cuts)))
        level = level * jnp.repeat(heights, shape[position] // parts).reshape([-1 if axis == position else 1 for axis in range(len(shape))])
    return level


def routed_block(key, own, number, rows, number_of, top, bound, slope):
    order = jax.random.permutation(key, number_of)
    heavy_load, common = shares(number_of, rows * top, bound, slope, True), shares(number_of, rows * top, bound, slope, False)
    places = jnp.arange(number_of)

    def named(sizes, offset_by):
        used = int((sizes > 0).sum())
        fixed = max(1, used // 4)
        shifted = fixed + (places - fixed + offset_by * (used - fixed)) % max(1, number_of - fixed)
        return jnp.zeros((number_of,), jnp.int32).at[order[jnp.where(places < fixed, places, shifted)]].set(jnp.asarray(sizes, jnp.int32))

    sizes = jnp.where(number % 4 == 0, named(heavy_load, number // 4), named(common, number - number // 4 - 1))
    mixed = jax.random.permutation(jax.random.fold_in(own, 3), number_of)
    donor, receiver = mixed[0:number_of // 2 * 2:2], mixed[1:number_of // 2 * 2:2]
    slack = jnp.minimum(sizes[donor] - 1, bound - sizes[receiver]) // 2
    slack = jnp.where((donor == order[0]) | (receiver == order[0]) | (sizes[receiver] == 0), 0, jnp.maximum(slack, 0))
    shifted = jax.random.randint(jax.random.fold_in(own, 4), (number_of // 2,), 0, 1 << 20) % (slack + 1)
    sizes = sizes.at[donor].add(-shifted).at[receiver].add(shifted)
    labels = jnp.searchsorted(jnp.cumsum(sizes), jnp.arange(rows * top), side="right").astype(jnp.int32)
    listing = labels.reshape(top, rows).T
    listing = listing[jax.random.permutation(jax.random.fold_in(own, 1), rows)]
    offset_by = jax.random.randint(jax.random.fold_in(own, 2), (rows, 1), 0, top)
    return jnp.take_along_axis(listing, (jnp.arange(top)[None, :] + offset_by) % top, axis=1)


def shares(amount, total, reach, slope, full):
    loads = [(1 << 20) // math.isqrt(standing ** slope) + 1 for standing in range(1, amount + 1)]
    largest = reach if full else min(reach, max(-(-total // amount), total * loads[0] // sum(loads)))
    least = 1 if total - largest >= amount - 1 else 0
    counts, surplus = [largest] + [least] * (amount - 1), total - largest - least * (amount - 1)
    while surplus > 0:
        free = [i for i in range(1, amount) if counts[i] < largest] or [i for i in range(1, amount) if counts[i] < reach]
        mass, left = sum([loads[i] for i in free]), surplus
        for i in free:
            extra = min(reach - counts[i], max(1, left * loads[i] // mass), surplus)
            counts[i] = counts[i] + extra
            surplus = surplus - extra
    return np.array(counts)


def noise(key, dims, scale, reach, cuts=(), kind=jnp.bfloat16):
    level = levels(key, dims, cuts, -0.22, 0.18) if cuts else 1.0
    values = jax.random.normal(key, dims, jnp.float32) * scale * level
    return jnp.minimum(jnp.maximum(values, -reach), reach).astype(kind)


def setup_inputs(seed: int = 0) -> dict:
    seeds = jax.random.split(jax.random.key(seed), 8)
    tokens = draw_tokens(jax.random.fold_in(seeds[7], 71), 0)
    norm_gain = jnp.clip(1.0 + 0.1 * jax.random.normal(seeds[1], (D,), jnp.float32), 0.5, 1.5)
    routes_keys = jax.random.split(jax.random.fold_in(seeds[2], 1), TOKENS // TOK_DEV)
    routes_turns = jax.random.permutation(jax.random.fold_in(seeds[2], 3), TOKENS // TOK_DEV)
    routes = jax.vmap(lambda own, number: routed_block(jax.random.fold_in(seeds[2], 2), own, number, TOK_DEV, EXPERTS, TOP, CAP, 1))(routes_keys, routes_turns).reshape((TOKENS, TOP))
    gate_weights = jnp.clip(0.05 + 0.95 * jax.random.uniform(seeds[3], (TOKENS, TOP), jnp.float32) ** levels(seeds[3], (TOKENS, TOP), ((0, 1024),), -0.2, 0.2), 0.05, 1.0)
    weight_in = noise(seeds[4], (EXPERTS, HID, D), D ** -0.5, 0.25, ((0, 64),))
    weight_out = noise(seeds[5], (EXPERTS, HID, D), HID ** -0.5, 0.125, ((0, 64),))
    out_grad = noise(seeds[6], (TOKENS, D), 0.25, 1.5, ((0, 1024),))
    return {"tokens": tokens, "norm_gain": norm_gain, "routes": routes, "gate_weights": gate_weights, "weight_in": weight_in, "weight_out": weight_out, "out_grad": out_grad}


epsilon = 1e-05

def swish_parts(hidden_v):
    sigmoid_v = jax.nn.sigmoid(hidden_v)
    return (hidden_v * sigmoid_v, sigmoid_v * (1.0 + hidden_v * (1.0 - sigmoid_v)))

def normalize(frames, norm_gain):
    values = frames.astype(jnp.float32)
    centered = values - lax.optimization_barrier(jnp.mean(values, axis=1, keepdims=True))
    inv_std = lax.rsqrt(lax.optimization_barrier(jnp.mean(centered * centered, axis=1, keepdims=True)) + epsilon)
    standard = centered * inv_std
    return (standard, inv_std, (standard * norm_gain).astype(jnp.bfloat16))

def slot_numbers(flat_exp):
    onehot = (flat_exp[:, None] == jnp.arange(EXPERTS, dtype=jnp.int32)[None, :]).astype(jnp.int32)
    before = jnp.cumsum(onehot, axis=0) - onehot
    return lax.optimization_barrier(jnp.sum(before * onehot, axis=1))

def expert_math(operands):
    rows_in, rows_cot, weight_in, weight_out = operands
    pre_act = jnp.dot(rows_in, weight_in.T, preferred_element_type=jnp.float32)
    act_full, derivative = swish_parts(pre_act)
    act_half = act_full.astype(jnp.bfloat16)
    expert_out = jnp.dot(act_half, weight_out, preferred_element_type=jnp.float32).astype(jnp.bfloat16)
    back_prod = jnp.dot(rows_cot, weight_out.T, preferred_element_type=jnp.float32)
    hid_grad = (back_prod * derivative).astype(jnp.bfloat16)
    in_grad = jnp.dot(hid_grad, weight_in, preferred_element_type=jnp.float32).astype(jnp.bfloat16)
    grad_in = jnp.dot(hid_grad.T, rows_in, preferred_element_type=jnp.float32)
    grad_out = jnp.dot(act_half.T, rows_cot, preferred_element_type=jnp.float32)
    return (expert_out, in_grad, grad_in, grad_out)

def group_pass(frames, route_ids, gate_w, cotangent, norm_gain, weight_in, weight_out):
    group_tok = frames.shape[0]
    standard, inv_std, normed = normalize(frames, norm_gain)
    scaled = (gate_w[:, :, None] * cotangent.astype(jnp.float32)[:, None, :]).astype(jnp.bfloat16)
    flat_exp = route_ids.reshape(EXPERTS, TOK_DEV * TOP)
    slot_of = jax.vmap(slot_numbers)(flat_exp)
    source = jnp.broadcast_to(jnp.arange(EXPERTS, dtype=jnp.int32)[:, None], flat_exp.shape)
    row_at = (source * CAP + slot_of).reshape(-1).astype(jnp.int32)
    expert_at = flat_exp.reshape(-1).astype(jnp.int32)
    rows_in = jnp.repeat(normed, TOP, axis=0)
    rows_cot = scaled.reshape(group_tok * TOP, D)
    buffer_in = jnp.zeros((EXPERTS, EXPERTS * CAP, D), jnp.bfloat16).at[expert_at, row_at].set(rows_in)
    buffer_cot = jnp.zeros((EXPERTS, EXPERTS * CAP, D), jnp.bfloat16).at[expert_at, row_at].set(rows_cot)
    outs, ins, grad_in, grad_out = lax.map(expert_math, (buffer_in, buffer_cot, weight_in, weight_out))
    y_rows = outs[expert_at, row_at].reshape(group_tok, TOP, D)
    du_rows = ins[expert_at, row_at].reshape(group_tok, TOP, D)
    mixed = lax.optimization_barrier(jnp.sum(gate_w[:, :, None] * y_rows.astype(jnp.float32), axis=1)).astype(jnp.bfloat16)
    gate_grad = jnp.einsum('td,tkd->tk', cotangent.astype(jnp.float32), y_rows.astype(jnp.float32))
    norm_grad = lax.optimization_barrier(jnp.sum(du_rows.astype(jnp.float32), axis=1)) * norm_gain
    token_grad = inv_std * (norm_grad - lax.optimization_barrier(jnp.mean(norm_grad, axis=1, keepdims=True)) - standard * lax.optimization_barrier(jnp.mean(norm_grad * standard, axis=1, keepdims=True)))
    return (mixed, gate_grad, token_grad.astype(jnp.bfloat16), grad_in, grad_out)

def reference(tokens, norm_gain, routes, gate_weights, weight_in, weight_out, out_grad):
    group_tok = TOK_DEV * EXPERTS

    def one_group(carry, operands):
        frames, route_ids, gate_w, cotangent = operands
        mixed, gate_grad, token_grad, grad_in, grad_out = group_pass(frames, route_ids, gate_w, cotangent, norm_gain, weight_in, weight_out)
        rounded_in = lax.optimization_barrier(grad_in.astype(jnp.bfloat16)).astype(jnp.float32)
        rounded_out = lax.optimization_barrier(grad_out.astype(jnp.bfloat16)).astype(jnp.float32)
        return ((carry[0] + rounded_in, carry[1] + rounded_out), (mixed, gate_grad, token_grad))
    start_sums = (jnp.zeros(weight_in.shape, jnp.float32), jnp.zeros(weight_out.shape, jnp.float32))
    grouped = (tokens.reshape(N_DP, group_tok, D), routes.reshape(N_DP, group_tok, TOP), gate_weights.reshape(N_DP, group_tok, TOP), out_grad.reshape(N_DP, group_tok, D))
    sums, stacked = lax.scan(one_group, start_sums, grouped)
    return (stacked[0].reshape(-1, D), stacked[1].reshape(-1, TOP), stacked[2].reshape(-1, D), sums[0], sums[1])
```

```python
import functools

import jax
import jax.numpy as jnp
from jax import lax
from jax.experimental import pallas as pl
from jax.experimental.pallas import tpu as pltpu
from jax.sharding import PartitionSpec as P

MESH = pl.DeviceIdType.MESH
EPS = 1e-05
CAP = 5
LANES = 128
NX = 4
CORES = 2
BF = jnp.bfloat16
F32 = jnp.float32


def ones_where(cond):
    return jnp.where(cond, 1.0, 0.0).astype(BF)


def fdot(a, b):
    return jnp.dot(a, b, preferred_element_type=F32)


def route_rows(shape, row_dim):
    r8 = lax.broadcasted_iota(jnp.int32, shape, row_dim)
    r5 = lax.broadcasted_iota(jnp.int32, shape, 1 - row_dim)
    base = lax.shift_right_logical(r8, 3) * CAP
    i = lax.bitwise_and(r8, 7)
    x_mask = jnp.where(i < CAP, base + i, -1) == r5
    c_mask = jnp.where(i >= CAP, base + i - CAP, -1) == r5
    f_row = base + 3 + lax.shift_right_logical(i, 2)
    g = lax.bitwise_and(i, 3)
    folds = [jnp.where(g == k, f_row, -1) == r5 for k in range(4)]
    return ones_where(x_mask), ones_where(c_mask), [ones_where(f) for f in folds]


def to_col(row, eye):
    return jnp.sum(jnp.where(eye, row, 0.0), axis=1, keepdims=True)


def kernel(
    cfg, tok_ref, gain_ref, routes_ref, gates_ref, win_ref, wout_ref, og_ref,
    mixed_ref, gg_ref, tg_ref, gin_ref, gout_ref,
    win, wout, send, recv, rsend, rrecv, rhs1, rhs2, std_ref,
    m1, m2, b1, b2, xs, cs, act, hg, gbuf, xbuf, sbuf, rbuf,
    w_sem, send_sem, recv_sem, rsend_sem, rrecv_sem, xs_sem, xr_sem, ss_sem, sr_sem,
):
    nz, ny, nch = cfg
    n_exp = NX * nz
    oc = n_exp // nch
    rows8, rows5 = oc * 8, oc * CAP
    frames, dim = tok_ref.shape
    ngrp = dim // LANES
    hid = win.shape[0]
    share = hid // (ny * CORES)
    half = ny // 2

    d = lax.axis_index("dp")
    e = lax.axis_index("expert")
    y, c = lax.div(d, CORES), lax.rem(d, CORES)
    x, z = lax.div(e, nz), lax.rem(e, nz)
    up = lax.rem(y + 1, ny) * CORES + c
    down = lax.rem(y + ny - 1, ny) * CORES + c
    mate = y * CORES + (1 - c)

    def offsets(o):
        p, xp = lax.div(o, NX), lax.rem(o, NX)
        odd = lax.rem(p, 2)
        dz = odd * lax.div(nz - 1 - p, 2) + (1 - odd) * lax.rem(nz // 2 + lax.div(p, 2), nz)
        return NX - 1 - xp, dz

    def peer_to(o):
        dx, dz = offsets(o)
        return (d, lax.rem(x + dx, NX) * nz + lax.rem(z + dz, nz))

    def peer_from(o):
        dx, dz = offsets(o)
        return (d, lax.rem(x + NX - dx, NX) * nz + lax.rem(z + nz - dz, nz))

    barrier = pltpu.get_barrier_semaphore()

    def greet(o, carry):
        pl.semaphore_signal(barrier, inc=1, device_id=peer_to(o), device_id_type=MESH)
        return carry

    lax.fori_loop(0, n_exp - 1, greet, 0)
    for other in (up, down, mate):
        pl.semaphore_signal(barrier, inc=1, device_id=(other, e), device_id_type=MESH)

    w_copies = [
        pltpu.make_async_copy(win_ref.at[0], win, w_sem.at[0]),
        pltpu.make_async_copy(wout_ref.at[0], wout, w_sem.at[1]),
    ]
    for copy in w_copies:
        copy.start()

    values = tok_ref[...].astype(F32)
    centered = values - jnp.mean(values, axis=1, keepdims=True)
    inv_std = lax.rsqrt(jnp.mean(centered * centered, axis=1, keepdims=True) + EPS)
    standard = centered * inv_std
    std_ref[...] = standard
    gain = gain_ref[...]
    rhs1[0:frames, :] = (standard * gain).astype(BF)

    f_row = lax.broadcasted_iota(jnp.int32, (frames, frames), 0)
    f_col = lax.broadcasted_iota(jnp.int32, (frames, frames), 1)
    eye = f_row == f_col
    og = og_ref[...].astype(F32)
    gates = [to_col(gates_ref[k : k + 1, :], eye) for k in range(2)]
    for k in range(2):
        scaled = (gates[k] * og).astype(BF)
        rhs1[frames * (k + 1) : frames * (k + 2), :] = scaled
        for g in range(ngrp):
            at = (k * ngrp + g) * frames
            rhs2[at : at + frames, :] = scaled[:, g * LANES : (g + 1) * LANES]

    rels, hots = [], []
    e_iota = lax.broadcasted_iota(jnp.int32, (n_exp, frames), 0)
    for k in range(2):
        r = routes_ref[k : k + 1, :]
        dx = lax.bitwise_and(lax.shift_right_logical(r, nz.bit_length() - 1) - x, NX - 1)
        dz = lax.bitwise_and(r - z, nz - 1)
        p = jnp.where(dz < nz // 2, nz - 1 - 2 * dz, 2 * dz - nz)
        rel = p * NX + (NX - 1 - dx)
        rels.append(rel)
        hots.append(jnp.where(e_iota == rel, 1.0, 0.0))
    before = fdot((hots[0] + hots[1]).astype(BF), ones_where(f_row < f_col))
    dest_a, dest_b, dest_f = [], [], []
    for k in range(2):
        slot = jnp.sum(hots[k] * before, axis=0, keepdims=True)
        base = rels[k].astype(F32) * 8.0
        dest_a.append(base + slot)
        dest_b.append(jnp.where(slot < 3.0, base + 5.0 + slot, -1.0))
        dest_f.append(jnp.where(slot >= 3.0, base + (slot - 3.0) * 4.0, -100.0))

    pl.semaphore_wait(barrier, n_exp + 2)

    def dispatch(o, q):
        return pltpu.make_async_remote_copy(
            src_ref=send.at[o], dst_ref=recv.at[o], send_sem=send_sem, recv_sem=recv_sem.at[q],
            device_id=peer_to(o), device_id_type=MESH,
        )

    def give_back(o, q):
        return pltpu.make_async_remote_copy(
            src_ref=rsend.at[o], dst_ref=rrecv.at[o], send_sem=rsend_sem, recv_sem=rrecv_sem.at[q],
            device_id=peer_from(o), device_id_type=MESH,
        )

    own = n_exp - 1

    def send_chunk(q, carry):
        rid = (lax.broadcasted_iota(jnp.int32, (rows8, frames), 0) + q * rows8).astype(F32)
        a = ones_where((rid == dest_a[0]) | (rid == dest_a[1]))
        lhs1 = jnp.concatenate([a] + [ones_where(rid == dest_b[k]) for k in range(2)], axis=1)
        lhs2 = jnp.concatenate(
            [ones_where(rid == dest_f[k] + float(g)) for k in range(2) for g in range(ngrp)], axis=1
        )
        first = q * oc
        send[pl.ds(first, oc), :, 0:dim] = fdot(lhs1, rhs1[...]).reshape(oc, 8, dim).astype(BF)
        send[pl.ds(first, oc), :, dim : dim + LANES] = (
            fdot(lhs2, rhs2[...]).reshape(oc, 8, LANES).astype(BF)
        )

        def start(i, carry):
            dispatch(first + i, q).start()
            return carry

        lax.fori_loop(0, jnp.where(q == nch - 1, oc - 1, oc), start, 0)
        return carry

    lax.fori_loop(0, nch, send_chunk, 0)
    own_copy = pltpu.make_async_copy(send.at[own], recv.at[own], recv_sem.at[nch - 1])
    own_copy.start()

    xm, cm, fm = route_rows((rows5, rows8), 1)
    m1[0:rows5, :] = xm
    m1[rows5 : 2 * rows5, :] = cm
    for g in range(ngrp):
        m2[g * rows5 : (g + 1) * rows5, :] = fm[g]
    xt, ct, ft = route_rows((rows8, rows5), 0)
    b1[...] = jnp.concatenate([xt, ct], axis=1)
    b2[...] = jnp.concatenate(ft, axis=1)

    for copy in w_copies:
        copy.wait()

    n_blk = 4
    blk = hid // n_blk
    nt = (((1,), (1,)), ((), ()))

    def expert_chunk(q, carry):
        first = q * oc
        row = pl.multiple_of(q * rows5, rows5)
        pltpu.make_async_copy(
            recv.at[pl.ds(first, oc)], recv.at[pl.ds(first, oc)], recv_sem.at[q]
        ).wait()
        msg = recv[pl.ds(first, oc)].astype(F32).reshape(rows8, dim + LANES).astype(BF)
        both = fdot(m1[...], msg[:, 0:dim])
        folded = fdot(m2[...], msg[:, dim : dim + LANES])
        x_in = both[0:rows5].astype(BF)
        fold_cat = jnp.concatenate(
            [folded[g * rows5 : (g + 1) * rows5] for g in range(ngrp)], axis=1
        )
        cot = (both[rows5 : 2 * rows5] + fold_cat).astype(BF)
        xs[pl.ds(row, rows5), :] = x_in
        cs[pl.ds(row, rows5), :] = cot
        out = jnp.zeros((rows5, dim), F32)
        ingrad = jnp.zeros((rows5, dim), F32)
        for b in range(n_blk):
            at = slice(b * blk, (b + 1) * blk)
            pre = lax.dot_general(x_in, win[at, :], nt, preferred_element_type=F32)
            back = lax.dot_general(cot, wout[at, :], nt, preferred_element_type=F32)
            sg = 0.5 * jnp.tanh(0.5 * pre) + 0.5
            act_b = (pre * sg).astype(BF)
            hg_b = (back * (sg * (1.0 + pre * (1.0 - sg)))).astype(BF)
            act[pl.ds(row, rows5), at] = act_b
            hg[pl.ds(row, rows5), at] = hg_b
            out = out + fdot(act_b, wout[at, :])
            ingrad = ingrad + fdot(hg_b, win[at, :])
        out_h, in_h = out.astype(BF), ingrad.astype(BF)
        rmain = fdot(b1[...], jnp.concatenate([out_h, in_h], axis=0))
        stack = jnp.concatenate(
            [in_h[:, g * LANES : (g + 1) * LANES] for g in range(ngrp)], axis=0
        )
        rfold = fdot(b2[...], stack)
        rsend[pl.ds(first, oc), :, 0:dim] = rmain.reshape(oc, 8, dim).astype(BF)
        rsend[pl.ds(first, oc), :, dim : dim + LANES] = rfold.reshape(oc, 8, LANES).astype(BF)

        def start(i, carry):
            give_back(first + i, q).start()
            return carry

        lax.fori_loop(0, jnp.where(q == nch - 1, oc - 1, oc), start, 0)
        return carry

    lax.fori_loop(0, nch, expert_chunk, 0)
    own_back = pltpu.make_async_copy(rsend.at[own], rrecv.at[own], rrecv_sem.at[nch - 1])
    own_back.start()

    tn = (((0,), (0,)), ((), ()))

    def exchange(j):
        return pltpu.make_async_remote_copy(
            src_ref=gbuf.at[j, :, pl.ds((1 - c) * share, share), :], dst_ref=xbuf.at[j],
            send_sem=xs_sem.at[j], recv_sem=xr_sem.at[j], device_id=(mate, e), device_id_type=MESH,
        )

    def grads(j):
        shift = half - (j + 1) // 2 if j % 2 else (half + j // 2) % ny
        at = pl.multiple_of(lax.rem(y + shift, ny) * (CORES * share), CORES * share)
        cols = pl.ds(at, CORES * share)
        gbuf[j, 0] = lax.dot_general(hg[:, cols], xs[...], tn, preferred_element_type=F32).astype(BF)
        gbuf[j, 1] = lax.dot_general(act[:, cols], cs[...], tn, preferred_element_type=F32).astype(BF)
        exchange(j).start()

    def term(j, part):
        mine = gbuf[j, part, pl.ds(pl.multiple_of(c * share, share), share), :].astype(F32)
        return mine + xbuf[j, part].astype(F32)

    def hop(way, step, part):
        return pltpu.make_async_remote_copy(
            src_ref=sbuf.at[way, step, part], dst_ref=rbuf.at[way, step, part],
            send_sem=ss_sem.at[way, step, part], recv_sem=sr_sem.at[way, step, part],
            device_id=((up, down)[way], e), device_id_type=MESH,
        )

    def parts_of(way, step):
        return ((way,) if step == 0 else (1 - way, way))

    hops = []
    grads(0)
    for step in range(half):
        js = (0,) if step == 0 else (2 * step - 1, 2 * step)
        ahead = [j for j in (2 * step + 1, 2 * step + 2) if j < ny]
        for j in ahead:
            grads(j)
        for j in js:
            exchange(j).wait_recv()
        order = (0, 1) if step == 1 or step == 0 else (0, 1)
        for i in order:
            for way in range(2):
                parts = parts_of(way, step)
                if i >= len(parts):
                    continue
                part = parts[i]
                j = js[way] if step else 0
                total = term(j, part)
                if step and part in parts_of(way, step - 1):
                    hop(way, step - 1, part).wait_recv()
                    total = total + rbuf[way, step - 1, part].astype(F32)
                sbuf[way, step, part] = total.astype(BF)
                copy = hop(way, step, part)
                copy.start()
                hops.append(copy)

    lane_id = lax.broadcasted_iota(jnp.int32, (frames, n_exp * 8), 1).astype(F32)
    cols_a = [to_col(dest_a[k], eye) for k in range(2)]
    cols_b = [to_col(dest_b[k], eye) for k in range(2)]
    cols_f = [to_col(dest_f[k], eye) for k in range(2)]
    pick_a = [ones_where(lane_id == cols_a[k]) for k in range(2)]
    pick_b = ones_where((lane_id == cols_b[0]) | (lane_id == cols_b[1]))
    pick_f = [
        ones_where((lane_id == cols_f[0] + float(g)) | (lane_id == cols_f[1] + float(g)))
        for g in range(ngrp)
    ]
    for q in range(nch):
        pltpu.make_async_copy(
            rrecv.at[pl.ds(q * oc, oc)], rrecv.at[pl.ds(q * oc, oc)], rrecv_sem.at[q]
        ).wait()
    msg = rrecv[...].astype(F32).reshape(n_exp * 8, dim + LANES).astype(BF)
    main, fold = msg[:, 0:dim], msg[:, dim : dim + LANES]
    og = og_ref[...].astype(F32)
    y_rows = [fdot(pick_a[k], main) for k in range(2)]
    mixed_ref[...] = (gates[0] * y_rows[0] + gates[1] * y_rows[1]).astype(BF)
    for k in range(2):
        dots = jnp.sum(og * y_rows[k], axis=1, keepdims=True)
        gg_ref[k : k + 1, :] = jnp.sum(jnp.where(eye, dots, 0.0), axis=0, keepdims=True)
    du = fdot(pick_b, main) + jnp.concatenate([fdot(pick_f[g], fold) for g in range(ngrp)], axis=1)
    norm_grad = du * gain
    standard = std_ref[...]
    tg_ref[...] = (
        inv_std
        * (
            norm_grad
            - jnp.mean(norm_grad, axis=1, keepdims=True)
            - standard * jnp.mean(norm_grad * standard, axis=1, keepdims=True)
        )
    ).astype(BF)

    last = half - 1
    exchange(ny - 1).wait_recv()
    for part, out_ref in ((0, gin_ref), (1, gout_ref)):
        total = term(ny - 1, part)
        for way in range(2):
            if part in parts_of(way, last):
                hop(way, last, part).wait_recv()
                total = total + rbuf[way, last, part].astype(F32)
        out_ref[0] = total

    pltpu.make_async_copy(send.at[pl.ds(0, own)], send.at[pl.ds(0, own)], send_sem).wait()
    pltpu.make_async_copy(rsend.at[pl.ds(0, own)], rsend.at[pl.ds(0, own)], rsend_sem).wait()
    for j in range(ny):
        exchange(j).wait_send()
    for copy in hops:
        copy.wait_send()


def local(nz, ny, nch, tokens, norm_gain, routes, gate_weights, weight_in, weight_out, out_grad):
    frames, dim = tokens.shape
    hid = weight_in.shape[1]
    n_exp = NX * nz
    oc = n_exp // nch
    share = hid // (ny * CORES)
    half = ny // 2
    ngrp = dim // LANES
    total = n_exp * CAP
    msgs = pltpu.VMEM((n_exp, 8, dim + LANES), BF)
    dma = pltpu.SemaphoreType.DMA
    vmem = pl.BlockSpec(memory_space=pltpu.VMEM)
    hbm = pl.BlockSpec(memory_space=pl.ANY)
    mixed, gate_grad, token_grad, gin, gout = pl.pallas_call(
        functools.partial(kernel, (nz, ny, nch)),
        out_shape=(
            jax.ShapeDtypeStruct((frames, dim), BF),
            jax.ShapeDtypeStruct((2, frames), F32),
            jax.ShapeDtypeStruct((frames, dim), BF),
            jax.ShapeDtypeStruct((1, share, dim), F32),
            jax.ShapeDtypeStruct((1, share, dim), F32),
        ),
        in_specs=[vmem, vmem, vmem, vmem, hbm, hbm, vmem],
        out_specs=(vmem,) * 5,
        scratch_shapes=[
            pltpu.VMEM((hid, dim), BF),
            pltpu.VMEM((hid, dim), BF),
            msgs, msgs, msgs, msgs,
            pltpu.VMEM((3 * frames, dim), BF),
            pltpu.VMEM((2 * ngrp * frames, LANES), BF),
            pltpu.VMEM((frames, dim), F32),
            pltpu.VMEM((2 * oc * CAP, oc * 8), BF),
            pltpu.VMEM((ngrp * oc * CAP, oc * 8), BF),
            pltpu.VMEM((oc * 8, 2 * oc * CAP), BF),
            pltpu.VMEM((oc * 8, ngrp * oc * CAP), BF),
            pltpu.VMEM((total, dim), BF),
            pltpu.VMEM((total, dim), BF),
            pltpu.VMEM((total, hid), BF),
            pltpu.VMEM((total, hid), BF),
            pltpu.VMEM((ny, 2, CORES * share, dim), BF),
            pltpu.VMEM((ny, 2, share, dim), BF),
            pltpu.VMEM((2, half, 2, share, dim), BF),
            pltpu.VMEM((2, half, 2, share, dim), BF),
            dma((2,)), dma, dma((nch,)), dma, dma((nch,)),
            dma((ny,)), dma((ny,)), dma((2, half, 2)), dma((2, half, 2)),
        ],
        compiler_params=pltpu.CompilerParams(
            collective_id=0, has_side_effects=True, vmem_limit_bytes=52 * 1024 * 1024
        ),
    )(
        tokens, norm_gain.reshape(1, dim), routes.T, gate_weights.T, weight_in, weight_out, out_grad
    )
    return mixed, gate_grad.T, token_grad, gin, gout


def solution(mesh):
    nz = mesh.shape["expert"] // NX
    ny = mesh.shape["dp"] // CORES
    frames = P(("dp", "expert"), None)
    weights = P("expert", None, None)
    return jax.shard_map(
        functools.partial(local, nz, ny, 4),
        mesh=mesh,
        in_specs=(frames, P(), frames, frames, weights, weights, frames),
        out_specs=(frames, frames, frames, P("expert", "dp", None), P("expert", "dp", None)),
        check_vma=False,
    )
```

```python
import functools

import jax
import jax.numpy as jnp
from jax import lax
from jax.experimental import pallas as pl
from jax.experimental.pallas import tpu as pltpu
from jax.sharding import PartitionSpec as P

MESH = pl.DeviceIdType.MESH
EPS = 1e-05
CAP = 5
LANES = 128
NX = 4
CORES = 2
DELAY = 2
VMEM_BYTES = 60 * 1024 * 1024
BF = jnp.bfloat16
F32 = jnp.float32


def ones_where(cond):
    return jnp.where(cond, 1.0, 0.0).astype(BF)


def fdot(a, b):
    return jnp.dot(a, b, preferred_element_type=F32)


def route_rows(shape, row_dim):
    r8 = lax.broadcasted_iota(jnp.int32, shape, row_dim)
    r5 = lax.broadcasted_iota(jnp.int32, shape, 1 - row_dim)
    base = lax.shift_right_logical(r8, 3) * CAP
    i = lax.bitwise_and(r8, 7)
    x_mask = jnp.where(i < CAP, base + i, -1) == r5
    c_mask = jnp.where(i >= CAP, base + i - CAP, -1) == r5
    f_row = base + 3 + lax.shift_right_logical(i, 2)
    g = lax.bitwise_and(i, 3)
    folds = [jnp.where(g == k, f_row, -1) == r5 for k in range(4)]
    return ones_where(x_mask), ones_where(c_mask), [ones_where(f) for f in folds]


def to_col(row, eye):
    return jnp.sum(jnp.where(eye, row, 0.0), axis=1, keepdims=True)


def kernel(
    cfg, tok_hbm, gain_hbm, routes_hbm, gates_hbm, win_ref, wout_ref, og_hbm,
    mixed_hbm, gg_hbm, tg_hbm, gin_hbm, gout_hbm,
    mixed_ref, gg_ref, tg_ref, gin_ref, gout_ref,
    tok_ref, gain_ref, routes_ref, gates_ref, og_ref,
    win, wout, send, recv, rsend, rrecv, rhs1, rhs2, std_ref,
    m1, m2, b1, b2, xs, cs, act, hg, gbuf, xbuf, sbuf, rbuf,
    in_sem, out_sem, w_sem, send_sem, recv_sem, rsend_sem, rrecv_sem, xs_sem, xr_sem, ss_sem, sr_sem,
):
    nz, ny, nch = cfg
    n_exp = NX * nz
    oc = n_exp // nch
    rows8, rows5 = oc * 8, oc * CAP
    frames, dim = tok_ref.shape
    ngrp = dim // LANES
    hid = win.shape[0]
    share = hid // (ny * CORES)
    half = ny // 2

    d = lax.axis_index("dp")
    e = lax.axis_index("expert")
    y, c = lax.div(d, CORES), lax.rem(d, CORES)
    x, z = lax.div(e, nz), lax.rem(e, nz)
    up = lax.rem(y + 1, ny) * CORES + c
    down = lax.rem(y + ny - 1, ny) * CORES + c
    mate = y * CORES + (1 - c)

    def offsets(o):
        p, xp = lax.div(o, NX), lax.rem(o, NX)
        odd = lax.rem(p, 2)
        dz = odd * lax.div(nz - 1 - p, 2) + (1 - odd) * lax.rem(nz // 2 + lax.div(p, 2), nz)
        return NX - 1 - xp, dz

    def peer_to(o):
        dx, dz = offsets(o)
        return (d, lax.rem(x + dx, NX) * nz + lax.rem(z + dz, nz))

    def peer_from(o):
        dx, dz = offsets(o)
        return (d, lax.rem(x + NX - dx, NX) * nz + lax.rem(z + nz - dz, nz))

    in_copies = [
        pltpu.make_async_copy(src, dst, in_sem.at[i])
        for i, (src, dst) in enumerate(
            (
                (routes_hbm, routes_ref),
                (gates_hbm, gates_ref),
                (tok_hbm, tok_ref),
                (gain_hbm, gain_ref),
                (og_hbm, og_ref),
            )
        )
    ]
    for copy in in_copies:
        copy.start()

    barrier = pltpu.get_barrier_semaphore()

    def greet(o, carry):
        pl.semaphore_signal(barrier, inc=1, device_id=peer_to(o), device_id_type=MESH)
        return carry

    lax.fori_loop(0, n_exp - 1, greet, 0)
    for other in (up, down, mate):
        pl.semaphore_signal(barrier, inc=1, device_id=(other, e), device_id_type=MESH)

    w_copies = [
        pltpu.make_async_copy(win_ref.at[0], win, w_sem.at[0]),
        pltpu.make_async_copy(wout_ref.at[0], wout, w_sem.at[1]),
    ]
    for copy in w_copies:
        copy.start()

    for copy in in_copies:
        copy.wait()
    values = tok_ref[...].astype(F32)
    centered = values - jnp.mean(values, axis=1, keepdims=True)
    inv_std = lax.rsqrt(jnp.mean(centered * centered, axis=1, keepdims=True) + EPS)
    standard = centered * inv_std
    std_ref[...] = standard
    gain = gain_ref[...]
    rhs1[0:frames, :] = (standard * gain).astype(BF)

    f_row = lax.broadcasted_iota(jnp.int32, (frames, frames), 0)
    f_col = lax.broadcasted_iota(jnp.int32, (frames, frames), 1)
    eye = f_row == f_col
    og = og_ref[...].astype(F32)
    gates = [to_col(gates_ref[k : k + 1, :], eye) for k in range(2)]
    for k in range(2):
        scaled = (gates[k] * og).astype(BF)
        rhs1[frames * (k + 1) : frames * (k + 2), :] = scaled
        for g in range(ngrp):
            at = (k * ngrp + g) * frames
            rhs2[at : at + frames, :] = scaled[:, g * LANES : (g + 1) * LANES]

    rels, hots = [], []
    e_iota = lax.broadcasted_iota(jnp.int32, (n_exp, frames), 0)
    for k in range(2):
        r = routes_ref[k : k + 1, :]
        dx = lax.bitwise_and(lax.shift_right_logical(r, nz.bit_length() - 1) - x, NX - 1)
        dz = lax.bitwise_and(r - z, nz - 1)
        p = jnp.where(dz < nz // 2, nz - 1 - 2 * dz, 2 * dz - nz)
        rel = p * NX + (NX - 1 - dx)
        rels.append(rel)
        hots.append(jnp.where(e_iota == rel, 1.0, 0.0))
    before = fdot((hots[0] + hots[1]).astype(BF), ones_where(f_row < f_col))
    dest_a, dest_b, dest_f = [], [], []
    for k in range(2):
        slot = jnp.sum(hots[k] * before, axis=0, keepdims=True)
        base = rels[k].astype(F32) * 8.0
        dest_a.append(base + slot)
        dest_b.append(jnp.where(slot < 3.0, base + 5.0 + slot, -1.0))
        dest_f.append(jnp.where(slot >= 3.0, base + (slot - 3.0) * 4.0, -100.0))

    pl.semaphore_wait(barrier, n_exp + 2)

    def dispatch(o, q):
        return pltpu.make_async_remote_copy(
            src_ref=send.at[o], dst_ref=recv.at[o], send_sem=send_sem, recv_sem=recv_sem.at[q],
            device_id=peer_to(o), device_id_type=MESH,
        )

    def give_back(o, q):
        return pltpu.make_async_remote_copy(
            src_ref=rsend.at[o], dst_ref=rrecv.at[o], send_sem=rsend_sem, recv_sem=rrecv_sem.at[q],
            device_id=peer_from(o), device_id_type=MESH,
        )

    own = n_exp - 1

    def send_chunk(q, carry):
        rid = (lax.broadcasted_iota(jnp.int32, (rows8, frames), 0) + q * rows8).astype(F32)
        a = ones_where((rid == dest_a[0]) | (rid == dest_a[1]))
        lhs1 = jnp.concatenate([a] + [ones_where(rid == dest_b[k]) for k in range(2)], axis=1)
        lhs2 = jnp.concatenate(
            [ones_where(rid == dest_f[k] + float(g)) for k in range(2) for g in range(ngrp)], axis=1
        )
        first = q * oc
        send[pl.ds(first, oc), :, 0:dim] = fdot(lhs1, rhs1[...]).reshape(oc, 8, dim).astype(BF)
        send[pl.ds(first, oc), :, dim : dim + LANES] = (
            fdot(lhs2, rhs2[...]).reshape(oc, 8, LANES).astype(BF)
        )

        def start(i, carry):
            dispatch(first + i, q).start()
            return carry

        lax.fori_loop(0, jnp.where(q == nch - 1, oc - 1, oc), start, 0)
        return carry

    lax.fori_loop(0, nch, send_chunk, 0)
    own_copy = pltpu.make_async_copy(send.at[own], recv.at[own], recv_sem.at[nch - 1])
    own_copy.start()

    xm, cm, fm = route_rows((rows5, rows8), 1)
    m1[0:rows5, :] = xm
    m1[rows5 : 2 * rows5, :] = cm
    for g in range(ngrp):
        m2[g * rows5 : (g + 1) * rows5, :] = fm[g]
    xt, ct, ft = route_rows((rows8, rows5), 0)
    b1[...] = jnp.concatenate([xt, ct], axis=1)
    b2[...] = jnp.concatenate(ft, axis=1)

    for copy in w_copies:
        copy.wait()

    n_blk = 4
    blk = hid // n_blk
    nt = (((1,), (1,)), ((), ()))

    def return_chunk(q):
        def start(i, carry):
            give_back(q * oc + i, q).start()
            return carry

        lax.fori_loop(0, jnp.where(q == nch - 1, oc - 1, oc), start, 0)

    def expert_chunk(q, carry):
        first = q * oc
        row = pl.multiple_of(q * rows5, rows5)
        pltpu.make_async_copy(
            recv.at[pl.ds(first, oc)], recv.at[pl.ds(first, oc)], recv_sem.at[q]
        ).wait()
        if DELAY:
            pl.when(q >= DELAY)(lambda: return_chunk(q - DELAY))
        msg = recv[pl.ds(first, oc)].astype(F32).reshape(rows8, dim + LANES).astype(BF)
        both = fdot(m1[...], msg[:, 0:dim])
        folded = fdot(m2[...], msg[:, dim : dim + LANES])
        x_in = both[0:rows5].astype(BF)
        fold_cat = jnp.concatenate(
            [folded[g * rows5 : (g + 1) * rows5] for g in range(ngrp)], axis=1
        )
        cot = (both[rows5 : 2 * rows5] + fold_cat).astype(BF)
        xs[pl.ds(row, rows5), :] = x_in
        cs[pl.ds(row, rows5), :] = cot
        out = jnp.zeros((rows5, dim), F32)
        ingrad = jnp.zeros((rows5, dim), F32)
        for b in range(n_blk):
            at = slice(b * blk, (b + 1) * blk)
            pre = lax.dot_general(x_in, win[at, :], nt, preferred_element_type=F32)
            back = lax.dot_general(cot, wout[at, :], nt, preferred_element_type=F32)
            sg = 0.5 * jnp.tanh(0.5 * pre) + 0.5
            act_b = (pre * sg).astype(BF)
            hg_b = (back * (sg * (1.0 + pre * (1.0 - sg)))).astype(BF)
            act[pl.ds(row, rows5), at] = act_b
            hg[pl.ds(row, rows5), at] = hg_b
            out = out + fdot(act_b, wout[at, :])
            ingrad = ingrad + fdot(hg_b, win[at, :])
        out_h, in_h = out.astype(BF), ingrad.astype(BF)
        rmain = fdot(b1[...], jnp.concatenate([out_h, in_h], axis=0))
        stack = jnp.concatenate(
            [in_h[:, g * LANES : (g + 1) * LANES] for g in range(ngrp)], axis=0
        )
        rfold = fdot(b2[...], stack)
        rsend[pl.ds(first, oc), :, 0:dim] = rmain.reshape(oc, 8, dim).astype(BF)
        rsend[pl.ds(first, oc), :, dim : dim + LANES] = rfold.reshape(oc, 8, LANES).astype(BF)

        return carry

    lax.fori_loop(0, nch, expert_chunk, 0)
    if DELAY:
        lax.fori_loop(nch - DELAY, nch, lambda q, carry: (return_chunk(q), carry)[1], 0)
    own_back = pltpu.make_async_copy(rsend.at[own], rrecv.at[own], rrecv_sem.at[nch - 1])
    own_back.start()

    tn = (((0,), (0,)), ((), ()))

    def exchange(j):
        return pltpu.make_async_remote_copy(
            src_ref=gbuf.at[j, :, pl.ds((1 - c) * share, share), :], dst_ref=xbuf.at[j],
            send_sem=xs_sem.at[j], recv_sem=xr_sem.at[j], device_id=(mate, e), device_id_type=MESH,
        )

    def grads(j):
        shift = half - (j + 1) // 2 if j % 2 else (half + j // 2) % ny
        at = pl.multiple_of(lax.rem(y + shift, ny) * (CORES * share), CORES * share)
        cols = pl.ds(at, CORES * share)
        gbuf[j, 0] = lax.dot_general(hg[:, cols], xs[...], tn, preferred_element_type=F32).astype(BF)
        gbuf[j, 1] = lax.dot_general(act[:, cols], cs[...], tn, preferred_element_type=F32).astype(BF)
        exchange(j).start()

    def term(j, part):
        mine = gbuf[j, part, pl.ds(pl.multiple_of(c * share, share), share), :].astype(F32)
        return mine + xbuf[j, part].astype(F32)

    def hop(way, step, part):
        return pltpu.make_async_remote_copy(
            src_ref=sbuf.at[way, step, part], dst_ref=rbuf.at[way, step, part],
            send_sem=ss_sem.at[way, step, part], recv_sem=sr_sem.at[way, step, part],
            device_id=((up, down)[way], e), device_id_type=MESH,
        )

    def parts_of(way, step):
        return ((way,) if step == 0 else (1 - way, way))

    hops = []
    grads(0)
    for step in range(half):
        js = (0,) if step == 0 else (2 * step - 1, 2 * step)
        ahead = [j for j in (2 * step + 1, 2 * step + 2) if j < ny]
        for j in ahead:
            grads(j)
        for j in js:
            exchange(j).wait_recv()
        order = (0, 1) if step == 1 or step == 0 else (0, 1)
        for i in order:
            for way in range(2):
                parts = parts_of(way, step)
                if i >= len(parts):
                    continue
                part = parts[i]
                j = js[way] if step else 0
                total = term(j, part)
                if step and part in parts_of(way, step - 1):
                    hop(way, step - 1, part).wait_recv()
                    total = total + rbuf[way, step - 1, part].astype(F32)
                sbuf[way, step, part] = total.astype(BF)
                copy = hop(way, step, part)
                copy.start()
                hops.append(copy)

    lane_id = lax.broadcasted_iota(jnp.int32, (frames, n_exp * 8), 1).astype(F32)
    cols_a = [to_col(dest_a[k], eye) for k in range(2)]
    cols_b = [to_col(dest_b[k], eye) for k in range(2)]
    cols_f = [to_col(dest_f[k], eye) for k in range(2)]
    pick_a = [ones_where(lane_id == cols_a[k]) for k in range(2)]
    pick_b = ones_where((lane_id == cols_b[0]) | (lane_id == cols_b[1]))
    pick_f = [
        ones_where((lane_id == cols_f[0] + float(g)) | (lane_id == cols_f[1] + float(g)))
        for g in range(ngrp)
    ]
    outs = [
        pltpu.make_async_copy(src, dst, out_sem.at[i])
        for i, (src, dst) in enumerate(
            (
                (mixed_ref, mixed_hbm),
                (gg_ref, gg_hbm),
                (tg_ref, tg_hbm),
                (gin_ref, gin_hbm),
                (gout_ref, gout_hbm),
            )
        )
    ]

    last = half - 1
    exchange(ny - 1).wait_recv()
    for part, out_ref in ((0, gin_ref), (1, gout_ref)):
        total = term(ny - 1, part)
        for way in range(2):
            if part in parts_of(way, last):
                hop(way, last, part).wait_recv()
                total = total + rbuf[way, last, part].astype(F32)
        out_ref[0] = total
        outs[3 + part].start()

    y_rows = [jnp.zeros((frames, dim), F32) for k in range(2)]
    du = jnp.zeros((frames, dim), F32)
    for q in range(nch):
        pltpu.make_async_copy(
            rrecv.at[pl.ds(q * oc, oc)], rrecv.at[pl.ds(q * oc, oc)], rrecv_sem.at[q]
        ).wait()
        msg = rrecv[q * oc : (q + 1) * oc].astype(F32).reshape(rows8, dim + LANES).astype(BF)
        main, fold = msg[:, 0:dim], msg[:, dim : dim + LANES]
        at = slice(q * rows8, (q + 1) * rows8)
        y_rows = [y_rows[k] + fdot(pick_a[k][:, at], main) for k in range(2)]
        folded = [fdot(pick_f[g][:, at], fold) for g in range(ngrp)]
        du = du + fdot(pick_b[:, at], main) + jnp.concatenate(folded, axis=1)
    og = og_ref[...].astype(F32)
    mixed_ref[...] = (gates[0] * y_rows[0] + gates[1] * y_rows[1]).astype(BF)
    for k in range(2):
        dots = jnp.sum(og * y_rows[k], axis=1, keepdims=True)
        gg_ref[k : k + 1, :] = jnp.sum(jnp.where(eye, dots, 0.0), axis=0, keepdims=True)
    norm_grad = du * gain
    standard = std_ref[...]
    tg_ref[...] = (
        inv_std
        * (
            norm_grad
            - jnp.mean(norm_grad, axis=1, keepdims=True)
            - standard * jnp.mean(norm_grad * standard, axis=1, keepdims=True)
        )
    ).astype(BF)

    for i in range(3):
        outs[i].start()

    pltpu.make_async_copy(send.at[pl.ds(0, own)], send.at[pl.ds(0, own)], send_sem).wait()
    pltpu.make_async_copy(rsend.at[pl.ds(0, own)], rsend.at[pl.ds(0, own)], rsend_sem).wait()
    for j in range(ny):
        exchange(j).wait_send()
    for copy in hops:
        copy.wait_send()
    for copy in outs:
        copy.wait()


def store_kernel(*refs):
    n = (len(refs) - 1) // 2
    copies = [
        pltpu.make_async_copy(refs[i], refs[n + i], refs[2 * n].at[i]) for i in range(n)
    ]
    for copy in copies:
        copy.start()
    for copy in copies:
        copy.wait()


def store(*arrays):
    return pl.pallas_call(
        store_kernel,
        out_shape=tuple(jax.ShapeDtypeStruct(a.shape, a.dtype) for a in arrays),
        in_specs=[pl.BlockSpec(memory_space=pltpu.VMEM)] * len(arrays),
        out_specs=(pl.BlockSpec(memory_space=pltpu.HBM),) * len(arrays),
        scratch_shapes=[pltpu.SemaphoreType.DMA((len(arrays),))],
        compiler_params=pltpu.CompilerParams(vmem_limit_bytes=VMEM_BYTES),
    )(*arrays)


def local(nz, ny, nch, tokens, norm_gain, routes, gate_weights, weight_in, weight_out, out_grad):
    frames, dim = tokens.shape
    hid = weight_in.shape[1]
    n_exp = NX * nz
    oc = n_exp // nch
    share = hid // (ny * CORES)
    half = ny // 2
    ngrp = dim // LANES
    total = n_exp * CAP
    msgs = pltpu.VMEM((n_exp, 8, dim + LANES), BF)
    dma = pltpu.SemaphoreType.DMA
    hbm = pl.BlockSpec(memory_space=pltpu.HBM)
    mixed, gate_grad, token_grad, gin, gout = pl.pallas_call(
        functools.partial(kernel, (nz, ny, nch)),
        out_shape=(
            jax.ShapeDtypeStruct((frames, dim), BF),
            jax.ShapeDtypeStruct((2, frames), F32),
            jax.ShapeDtypeStruct((frames, dim), BF),
            jax.ShapeDtypeStruct((1, share, dim), F32),
            jax.ShapeDtypeStruct((1, share, dim), F32),
        ),
        in_specs=[hbm] * 7,
        out_specs=(hbm,) * 5,
        scratch_shapes=[
            pltpu.VMEM((frames, dim), BF),
            pltpu.VMEM((2, frames), F32),
            pltpu.VMEM((frames, dim), BF),
            pltpu.VMEM((1, share, dim), F32),
            pltpu.VMEM((1, share, dim), F32),
            pltpu.VMEM((frames, dim), BF),
            pltpu.VMEM((1, dim), F32),
            pltpu.VMEM((2, frames), jnp.int32),
            pltpu.VMEM((2, frames), F32),
            pltpu.VMEM((frames, dim), BF),
            pltpu.VMEM((hid, dim), BF),
            pltpu.VMEM((hid, dim), BF),
            msgs, msgs, msgs, msgs,
            pltpu.VMEM((3 * frames, dim), BF),
            pltpu.VMEM((2 * ngrp * frames, LANES), BF),
            pltpu.VMEM((frames, dim), F32),
            pltpu.VMEM((2 * oc * CAP, oc * 8), BF),
            pltpu.VMEM((ngrp * oc * CAP, oc * 8), BF),
            pltpu.VMEM((oc * 8, 2 * oc * CAP), BF),
            pltpu.VMEM((oc * 8, ngrp * oc * CAP), BF),
            pltpu.VMEM((total, dim), BF),
            pltpu.VMEM((total, dim), BF),
            pltpu.VMEM((total, hid), BF),
            pltpu.VMEM((total, hid), BF),
            pltpu.VMEM((ny, 2, CORES * share, dim), BF),
            pltpu.VMEM((ny, 2, share, dim), BF),
            pltpu.VMEM((2, half, 2, share, dim), BF),
            pltpu.VMEM((2, half, 2, share, dim), BF),
            dma((5,)), dma((5,)), dma((2,)), dma, dma((nch,)), dma, dma((nch,)),
            dma((ny,)), dma((ny,)), dma((2, half, 2)), dma((2, half, 2)),
        ],
        compiler_params=pltpu.CompilerParams(
            collective_id=0, has_side_effects=True, vmem_limit_bytes=VMEM_BYTES
        ),
    )(
        tokens, norm_gain.reshape(1, dim), routes.T, gate_weights.T, weight_in, weight_out, out_grad
    )
    mixed, gate_grad, token_grad, gin, gout = store(mixed, gate_grad, token_grad, gin, gout)
    return mixed, gate_grad.T, token_grad, gin, gout


def solution(mesh):
    nz = mesh.shape["expert"] // NX
    ny = mesh.shape["dp"] // CORES
    frames = P(("dp", "expert"), None)
    weights = P("expert", None, None)
    return jax.shard_map(
        functools.partial(local, nz, ny, 4),
        mesh=mesh,
        in_specs=(frames, P(), frames, frames, weights, weights, frames),
        out_specs=(frames, frames, frames, P("expert", "dp", None), P("expert", "dp", None)),
        check_vma=False,
    )
```

```python
import functools

import jax
import jax.numpy as jnp
from jax import lax
from jax.experimental import pallas as pl
from jax.experimental.pallas import tpu as pltpu
from jax.sharding import PartitionSpec as P

MESH = pl.DeviceIdType.MESH
EPS = 1e-05
CAP = 5
LANES = 128
NX = 4
CORES = 2
DELAY = 2
VMEM_BYTES = 60 * 1024 * 1024
BF = jnp.bfloat16
F32 = jnp.float32


def ones_where(cond):
    return jnp.where(cond, 1.0, 0.0).astype(BF)


def fdot(a, b):
    return jnp.dot(a, b, preferred_element_type=F32)


def route_rows(shape, row_dim):
    r8 = lax.broadcasted_iota(jnp.int32, shape, row_dim)
    r5 = lax.broadcasted_iota(jnp.int32, shape, 1 - row_dim)
    base = lax.shift_right_logical(r8, 3) * CAP
    i = lax.bitwise_and(r8, 7)
    x_mask = jnp.where(i < CAP, base + i, -1) == r5
    c_mask = jnp.where(i >= CAP, base + i - CAP, -1) == r5
    f_row = base + 3 + lax.shift_right_logical(i, 2)
    g = lax.bitwise_and(i, 3)
    folds = [jnp.where(g == k, f_row, -1) == r5 for k in range(4)]
    return ones_where(x_mask), ones_where(c_mask), [ones_where(f) for f in folds]


def to_col(row, eye):
    return jnp.sum(jnp.where(eye, row, 0.0), axis=1, keepdims=True)


def kernel(
    cfg, tok_hbm, gain_hbm, routes_hbm, gates_hbm, win_ref, wout_ref, og_hbm,
    mixed_hbm, gg_hbm, tg_hbm, gin_hbm, gout_hbm,
    mixed_ref, gg_ref, tg_ref, gin_ref, gout_ref,
    tok_ref, gain_ref, routes_ref, gates_ref, og_ref,
    win, wout, send, recv, rsend, rrecv, rhs1, rhs2, std_ref,
    m1, m2, b1, b2, xs, cs, act, hg, gbuf, xbuf, sbuf, rbuf,
    in_sem, out_sem, w_sem, send_sem, recv_sem, rsend_sem, rrecv_sem, xs_sem, xr_sem, ss_sem, sr_sem,
):
    nz, ny, nch = cfg
    n_exp = NX * nz
    oc = n_exp // nch
    rows8, rows5 = oc * 8, oc * CAP
    frames, dim = tok_ref.shape
    ngrp = dim // LANES
    hid = win.shape[0]
    share = hid // (ny * CORES)
    half = ny // 2

    d = lax.axis_index("dp")
    e = lax.axis_index("expert")
    y, c = lax.div(d, CORES), lax.rem(d, CORES)
    x, z = lax.div(e, nz), lax.rem(e, nz)
    up = lax.rem(y + 1, ny) * CORES + c
    down = lax.rem(y + ny - 1, ny) * CORES + c
    mate = y * CORES + (1 - c)

    def column(p):
        odd = lax.rem(p, 2)
        return odd * lax.div(nz - 1 - p, 2) + (1 - odd) * lax.rem(nz // 2 + lax.div(p, 2), nz)

    to_x = [lax.rem(x + NX - 1 - xp, NX) * nz for xp in range(NX)]
    from_x = [lax.rem(x + 1 + xp, NX) * nz for xp in range(NX)]

    def to_z(p):
        return lax.rem(z + column(p), nz)

    def from_z(p):
        return lax.rem(z + nz - column(p), nz)

    def each_peer(first, last, act):
        def columns(p, carry):
            for xp in range(NX):
                act(p, xp)
            return carry

        lax.fori_loop(first, jnp.minimum(last, nz - 1), columns, 0)

        def rest():
            for xp in range(NX - 1):
                act(nz - 1, xp)

        if isinstance(last, int):
            rest()
        else:
            pl.when(last == nz)(rest)

    in_copies = [
        pltpu.make_async_copy(src, dst, in_sem.at[i])
        for i, (src, dst) in enumerate(
            (
                (routes_hbm, routes_ref),
                (gates_hbm, gates_ref),
                (tok_hbm, tok_ref),
                (gain_hbm, gain_ref),
                (og_hbm, og_ref),
            )
        )
    ]
    for copy in in_copies:
        copy.start()

    barrier = pltpu.get_barrier_semaphore()

    def greet(p, xp):
        pl.semaphore_signal(
            barrier, inc=1, device_id=(d, to_x[xp] + to_z(p)), device_id_type=MESH
        )

    each_peer(0, nz, greet)
    for other in (up, down, mate):
        pl.semaphore_signal(barrier, inc=1, device_id=(other, e), device_id_type=MESH)

    w_copies = [
        pltpu.make_async_copy(win_ref.at[0], win, w_sem.at[0]),
        pltpu.make_async_copy(wout_ref.at[0], wout, w_sem.at[1]),
    ]
    for copy in w_copies:
        copy.start()

    for copy in in_copies:
        copy.wait()
    values = tok_ref[...].astype(F32)
    centered = values - jnp.mean(values, axis=1, keepdims=True)
    inv_std = lax.rsqrt(jnp.mean(centered * centered, axis=1, keepdims=True) + EPS)
    standard = centered * inv_std
    std_ref[...] = standard
    gain = gain_ref[...]
    rhs1[0:frames, :] = (standard * gain).astype(BF)

    f_row = lax.broadcasted_iota(jnp.int32, (frames, frames), 0)
    f_col = lax.broadcasted_iota(jnp.int32, (frames, frames), 1)
    eye = f_row == f_col
    og = og_ref[...].astype(F32)
    gates = [to_col(gates_ref[k : k + 1, :], eye) for k in range(2)]
    for k in range(2):
        scaled = (gates[k] * og).astype(BF)
        rhs1[frames * (k + 1) : frames * (k + 2), :] = scaled
        for g in range(ngrp):
            at = (k * ngrp + g) * frames
            rhs2[at : at + frames, :] = scaled[:, g * LANES : (g + 1) * LANES]

    rels, hots = [], []
    e_iota = lax.broadcasted_iota(jnp.int32, (n_exp, frames), 0)
    for k in range(2):
        r = routes_ref[k : k + 1, :]
        dx = lax.bitwise_and(lax.shift_right_logical(r, nz.bit_length() - 1) - x, NX - 1)
        dz = lax.bitwise_and(r - z, nz - 1)
        p = jnp.where(dz < nz // 2, nz - 1 - 2 * dz, 2 * dz - nz)
        rel = p * NX + (NX - 1 - dx)
        rels.append(rel)
        hots.append(jnp.where(e_iota == rel, 1.0, 0.0))
    before = fdot((hots[0] + hots[1]).astype(BF), ones_where(f_row < f_col))
    dest_a, dest_b, dest_f = [], [], []
    for k in range(2):
        slot = jnp.sum(hots[k] * before, axis=0, keepdims=True)
        base = rels[k].astype(F32) * 8.0
        dest_a.append(base + slot)
        dest_b.append(jnp.where(slot < 3.0, base + 5.0 + slot, -1.0))
        dest_f.append(jnp.where(slot >= 3.0, base + (slot - 3.0) * 4.0, -100.0))

    pl.semaphore_wait(barrier, n_exp + 2)

    def dispatch(q, p, xp):
        o = p * NX + xp
        pltpu.make_async_remote_copy(
            src_ref=send.at[o], dst_ref=recv.at[o], send_sem=send_sem, recv_sem=recv_sem.at[q],
            device_id=(d, to_x[xp] + to_z(p)), device_id_type=MESH,
        ).start()

    def give_back(q, p, xp):
        o = p * NX + xp
        pltpu.make_async_remote_copy(
            src_ref=rsend.at[o], dst_ref=rrecv.at[o], send_sem=rsend_sem, recv_sem=rrecv_sem.at[q],
            device_id=(d, from_x[xp] + from_z(p)), device_id_type=MESH,
        ).start()

    grp = nz // nch
    own = n_exp - 1

    def send_chunk(q, carry):
        rid = (lax.broadcasted_iota(jnp.int32, (rows8, frames), 0) + q * rows8).astype(F32)
        a = ones_where((rid == dest_a[0]) | (rid == dest_a[1]))
        lhs1 = jnp.concatenate([a] + [ones_where(rid == dest_b[k]) for k in range(2)], axis=1)
        lhs2 = jnp.concatenate(
            [ones_where(rid == dest_f[k] + float(g)) for k in range(2) for g in range(ngrp)], axis=1
        )
        first = q * oc
        send[pl.ds(first, oc), :, 0:dim] = fdot(lhs1, rhs1[...]).reshape(oc, 8, dim).astype(BF)
        send[pl.ds(first, oc), :, dim : dim + LANES] = (
            fdot(lhs2, rhs2[...]).reshape(oc, 8, LANES).astype(BF)
        )

        each_peer(q * grp, q * grp + grp, functools.partial(dispatch, q))
        return carry

    lax.fori_loop(0, nch, send_chunk, 0)
    own_copy = pltpu.make_async_copy(send.at[own], recv.at[own], recv_sem.at[nch - 1])
    own_copy.start()

    xm, cm, fm = route_rows((rows5, rows8), 1)
    m1[0:rows5, :] = xm
    m1[rows5 : 2 * rows5, :] = cm
    for g in range(ngrp):
        m2[g * rows5 : (g + 1) * rows5, :] = fm[g]
    xt, ct, ft = route_rows((rows8, rows5), 0)
    b1[...] = jnp.concatenate([xt, ct], axis=1)
    b2[...] = jnp.concatenate(ft, axis=1)

    for copy in w_copies:
        copy.wait()

    n_blk = 4
    blk = hid // n_blk
    nt = (((1,), (1,)), ((), ()))

    def return_chunk(q):
        each_peer(q * grp, q * grp + grp, functools.partial(give_back, q))

    def expert_chunk(q, carry):
        first = q * oc
        row = pl.multiple_of(q * rows5, rows5)
        pltpu.make_async_copy(
            recv.at[pl.ds(first, oc)], recv.at[pl.ds(first, oc)], recv_sem.at[q]
        ).wait()
        if DELAY:
            pl.when(q >= DELAY)(lambda: return_chunk(q - DELAY))
        msg = recv[pl.ds(first, oc)].astype(F32).reshape(rows8, dim + LANES).astype(BF)
        both = fdot(m1[...], msg[:, 0:dim])
        folded = fdot(m2[...], msg[:, dim : dim + LANES])
        x_in = both[0:rows5].astype(BF)
        fold_cat = jnp.concatenate(
            [folded[g * rows5 : (g + 1) * rows5] for g in range(ngrp)], axis=1
        )
        cot = (both[rows5 : 2 * rows5] + fold_cat).astype(BF)
        xs[pl.ds(row, rows5), :] = x_in
        cs[pl.ds(row, rows5), :] = cot
        out = jnp.zeros((rows5, dim), F32)
        ingrad = jnp.zeros((rows5, dim), F32)
        for b in range(n_blk):
            at = slice(b * blk, (b + 1) * blk)
            pre = lax.dot_general(x_in, win[at, :], nt, preferred_element_type=F32)
            back = lax.dot_general(cot, wout[at, :], nt, preferred_element_type=F32)
            sg = 0.5 * jnp.tanh(0.5 * pre) + 0.5
            act_b = (pre * sg).astype(BF)
            hg_b = (back * (sg * (1.0 + pre * (1.0 - sg)))).astype(BF)
            act[pl.ds(row, rows5), at] = act_b
            hg[pl.ds(row, rows5), at] = hg_b
            out = out + fdot(act_b, wout[at, :])
            ingrad = ingrad + fdot(hg_b, win[at, :])
        out_h, in_h = out.astype(BF), ingrad.astype(BF)
        rmain = fdot(b1[...], jnp.concatenate([out_h, in_h], axis=0))
        stack = jnp.concatenate(
            [in_h[:, g * LANES : (g + 1) * LANES] for g in range(ngrp)], axis=0
        )
        rfold = fdot(b2[...], stack)
        rsend[pl.ds(first, oc), :, 0:dim] = rmain.reshape(oc, 8, dim).astype(BF)
        rsend[pl.ds(first, oc), :, dim : dim + LANES] = rfold.reshape(oc, 8, LANES).astype(BF)

        return carry

    lax.fori_loop(0, nch, expert_chunk, 0)
    if DELAY:
        lax.fori_loop(nch - DELAY, nch, lambda q, carry: (return_chunk(q), carry)[1], 0)
    own_back = pltpu.make_async_copy(rsend.at[own], rrecv.at[own], rrecv_sem.at[nch - 1])
    own_back.start()

    tn = (((0,), (0,)), ((), ()))

    def exchange(j):
        return pltpu.make_async_remote_copy(
            src_ref=gbuf.at[j, :, pl.ds((1 - c) * share, share), :], dst_ref=xbuf.at[j],
            send_sem=xs_sem.at[j], recv_sem=xr_sem.at[j], device_id=(mate, e), device_id_type=MESH,
        )

    def grads(j):
        shift = half - (j + 1) // 2 if j % 2 else (half + j // 2) % ny
        at = pl.multiple_of(lax.rem(y + shift, ny) * (CORES * share), CORES * share)
        cols = pl.ds(at, CORES * share)
        gbuf[j, 0] = lax.dot_general(hg[:, cols], xs[...], tn, preferred_element_type=F32).astype(BF)
        gbuf[j, 1] = lax.dot_general(act[:, cols], cs[...], tn, preferred_element_type=F32).astype(BF)
        exchange(j).start()

    def term(j, part):
        mine = gbuf[j, part, pl.ds(pl.multiple_of(c * share, share), share), :].astype(F32)
        return mine + xbuf[j, part].astype(F32)

    def hop(way, step, part):
        return pltpu.make_async_remote_copy(
            src_ref=sbuf.at[way, step, part], dst_ref=rbuf.at[way, step, part],
            send_sem=ss_sem.at[way, step, part], recv_sem=sr_sem.at[way, step, part],
            device_id=((up, down)[way], e), device_id_type=MESH,
        )

    def parts_of(way, step):
        return ((way,) if step == 0 else (1 - way, way))

    hops = []
    grads(0)
    for step in range(half):
        js = (0,) if step == 0 else (2 * step - 1, 2 * step)
        ahead = [j for j in (2 * step + 1, 2 * step + 2) if j < ny]
        for j in ahead:
            grads(j)
        for j in js:
            exchange(j).wait_recv()
        order = (0, 1) if step == 1 or step == 0 else (0, 1)
        for i in order:
            for way in range(2):
                parts = parts_of(way, step)
                if i >= len(parts):
                    continue
                part = parts[i]
                j = js[way] if step else 0
                total = term(j, part)
                if step and part in parts_of(way, step - 1):
                    hop(way, step - 1, part).wait_recv()
                    total = total + rbuf[way, step - 1, part].astype(F32)
                sbuf[way, step, part] = total.astype(BF)
                copy = hop(way, step, part)
                copy.start()
                hops.append(copy)

    lane_id = lax.broadcasted_iota(jnp.int32, (frames, n_exp * 8), 1).astype(F32)
    cols_a = [to_col(dest_a[k], eye) for k in range(2)]
    cols_b = [to_col(dest_b[k], eye) for k in range(2)]
    cols_f = [to_col(dest_f[k], eye) for k in range(2)]
    pick_a = [ones_where(lane_id == cols_a[k]) for k in range(2)]
    pick_b = ones_where((lane_id == cols_b[0]) | (lane_id == cols_b[1]))
    pick_f = [
        ones_where((lane_id == cols_f[0] + float(g)) | (lane_id == cols_f[1] + float(g)))
        for g in range(ngrp)
    ]
    outs = [
        pltpu.make_async_copy(src, dst, out_sem.at[i])
        for i, (src, dst) in enumerate(
            (
                (mixed_ref, mixed_hbm),
                (gg_ref, gg_hbm),
                (tg_ref, tg_hbm),
                (gin_ref, gin_hbm),
                (gout_ref, gout_hbm),
            )
        )
    ]

    last = half - 1
    exchange(ny - 1).wait_recv()
    for part, out_ref in ((0, gin_ref), (1, gout_ref)):
        total = term(ny - 1, part)
        for way in range(2):
            if part in parts_of(way, last):
                hop(way, last, part).wait_recv()
                total = total + rbuf[way, last, part].astype(F32)
        out_ref[0] = total
        outs[3 + part].start()

    y_rows = [jnp.zeros((frames, dim), F32) for k in range(2)]
    du = jnp.zeros((frames, dim), F32)
    for q in range(nch):
        pltpu.make_async_copy(
            rrecv.at[pl.ds(q * oc, oc)], rrecv.at[pl.ds(q * oc, oc)], rrecv_sem.at[q]
        ).wait()
        msg = rrecv[q * oc : (q + 1) * oc].astype(F32).reshape(rows8, dim + LANES).astype(BF)
        main, fold = msg[:, 0:dim], msg[:, dim : dim + LANES]
        at = slice(q * rows8, (q + 1) * rows8)
        y_rows = [y_rows[k] + fdot(pick_a[k][:, at], main) for k in range(2)]
        folded = [fdot(pick_f[g][:, at], fold) for g in range(ngrp)]
        du = du + fdot(pick_b[:, at], main) + jnp.concatenate(folded, axis=1)
    og = og_ref[...].astype(F32)
    mixed_ref[...] = (gates[0] * y_rows[0] + gates[1] * y_rows[1]).astype(BF)
    for k in range(2):
        dots = jnp.sum(og * y_rows[k], axis=1, keepdims=True)
        gg_ref[k : k + 1, :] = jnp.sum(jnp.where(eye, dots, 0.0), axis=0, keepdims=True)
    norm_grad = du * gain
    standard = std_ref[...]
    tg_ref[...] = (
        inv_std
        * (
            norm_grad
            - jnp.mean(norm_grad, axis=1, keepdims=True)
            - standard * jnp.mean(norm_grad * standard, axis=1, keepdims=True)
        )
    ).astype(BF)

    for i in range(3):
        outs[i].start()

    pltpu.make_async_copy(send.at[pl.ds(0, own)], send.at[pl.ds(0, own)], send_sem).wait()
    pltpu.make_async_copy(rsend.at[pl.ds(0, own)], rsend.at[pl.ds(0, own)], rsend_sem).wait()
    for j in range(ny):
        exchange(j).wait_send()
    for copy in hops:
        copy.wait_send()
    for copy in outs:
        copy.wait()


def store_kernel(*refs):
    n = (len(refs) - 1) // 2
    copies = [
        pltpu.make_async_copy(refs[i], refs[n + i], refs[2 * n].at[i]) for i in range(n)
    ]
    for copy in copies:
        copy.start()
    for copy in copies:
        copy.wait()


def store(*arrays):
    return pl.pallas_call(
        store_kernel,
        out_shape=tuple(jax.ShapeDtypeStruct(a.shape, a.dtype) for a in arrays),
        in_specs=[pl.BlockSpec(memory_space=pltpu.VMEM)] * len(arrays),
        out_specs=(pl.BlockSpec(memory_space=pltpu.HBM),) * len(arrays),
        scratch_shapes=[pltpu.SemaphoreType.DMA((len(arrays),))],
        compiler_params=pltpu.CompilerParams(vmem_limit_bytes=VMEM_BYTES),
    )(*arrays)


def local(nz, ny, nch, tokens, norm_gain, routes, gate_weights, weight_in, weight_out, out_grad):
    frames, dim = tokens.shape
    hid = weight_in.shape[1]
    n_exp = NX * nz
    oc = n_exp // nch
    share = hid // (ny * CORES)
    half = ny // 2
    ngrp = dim // LANES
    total = n_exp * CAP
    msgs = pltpu.VMEM((n_exp, 8, dim + LANES), BF)
    dma = pltpu.SemaphoreType.DMA
    hbm = pl.BlockSpec(memory_space=pltpu.HBM)
    mixed, gate_grad, token_grad, gin, gout = pl.pallas_call(
        functools.partial(kernel, (nz, ny, nch)),
        out_shape=(
            jax.ShapeDtypeStruct((frames, dim), BF),
            jax.ShapeDtypeStruct((2, frames), F32),
            jax.ShapeDtypeStruct((frames, dim), BF),
            jax.ShapeDtypeStruct((1, share, dim), F32),
            jax.ShapeDtypeStruct((1, share, dim), F32),
        ),
        in_specs=[hbm] * 7,
        out_specs=(hbm,) * 5,
        scratch_shapes=[
            pltpu.VMEM((frames, dim), BF),
            pltpu.VMEM((2, frames), F32),
            pltpu.VMEM((frames, dim), BF),
            pltpu.VMEM((1, share, dim), F32),
            pltpu.VMEM((1, share, dim), F32),
            pltpu.VMEM((frames, dim), BF),
            pltpu.VMEM((1, dim), F32),
            pltpu.VMEM((2, frames), jnp.int32),
            pltpu.VMEM((2, frames), F32),
            pltpu.VMEM((frames, dim), BF),
            pltpu.VMEM((hid, dim), BF),
            pltpu.VMEM((hid, dim), BF),
            msgs, msgs, msgs, msgs,
            pltpu.VMEM((3 * frames, dim), BF),
            pltpu.VMEM((2 * ngrp * frames, LANES), BF),
            pltpu.VMEM((frames, dim), F32),
            pltpu.VMEM((2 * oc * CAP, oc * 8), BF),
            pltpu.VMEM((ngrp * oc * CAP, oc * 8), BF),
            pltpu.VMEM((oc * 8, 2 * oc * CAP), BF),
            pltpu.VMEM((oc * 8, ngrp * oc * CAP), BF),
            pltpu.VMEM((total, dim), BF),
            pltpu.VMEM((total, dim), BF),
            pltpu.VMEM((total, hid), BF),
            pltpu.VMEM((total, hid), BF),
            pltpu.VMEM((ny, 2, CORES * share, dim), BF),
            pltpu.VMEM((ny, 2, share, dim), BF),
            pltpu.VMEM((2, half, 2, share, dim), BF),
            pltpu.VMEM((2, half, 2, share, dim), BF),
            dma((5,)), dma((5,)), dma((2,)), dma, dma((nch,)), dma, dma((nch,)),
            dma((ny,)), dma((ny,)), dma((2, half, 2)), dma((2, half, 2)),
        ],
        compiler_params=pltpu.CompilerParams(
            collective_id=0, has_side_effects=True, vmem_limit_bytes=VMEM_BYTES
        ),
    )(
        tokens, norm_gain.reshape(1, dim), routes.T, gate_weights.T, weight_in, weight_out, out_grad
    )
    mixed, gate_grad, token_grad, gin, gout = store(mixed, gate_grad, token_grad, gin, gout)
    return mixed, gate_grad.T, token_grad, gin, gout


def solution(mesh):
    nz = mesh.shape["expert"] // NX
    ny = mesh.shape["dp"] // CORES
    frames = P(("dp", "expert"), None)
    weights = P("expert", None, None)
    return jax.shard_map(
        functools.partial(local, nz, ny, 4),
        mesh=mesh,
        in_specs=(frames, P(), frames, frames, weights, weights, frames),
        out_specs=(frames, frames, frames, P("expert", "dp", None), P("expert", "dp", None)),
        check_vma=False,
    )
```

```python
import functools

import jax
import jax.numpy as jnp
from jax import lax
from jax.experimental import pallas as pl
from jax.experimental.pallas import tpu as pltpu
from jax.sharding import PartitionSpec as P

MESH = pl.DeviceIdType.MESH
EPS = 1e-05
CAP = 5
LANES = 128
NX = 4
CORES = 2
DELAY = 2
VMEM_BYTES = 60 * 1024 * 1024
BF = jnp.bfloat16
F32 = jnp.float32


def ones_where(cond):
    return jnp.where(cond, 1.0, 0.0).astype(BF)


def fdot(a, b):
    return jnp.dot(a, b, preferred_element_type=F32)


def route_rows(shape, row_dim):
    r8 = lax.broadcasted_iota(jnp.int32, shape, row_dim)
    r5 = lax.broadcasted_iota(jnp.int32, shape, 1 - row_dim)
    base = lax.shift_right_logical(r8, 3) * CAP
    i = lax.bitwise_and(r8, 7)
    x_mask = jnp.where(i < CAP, base + i, -1) == r5
    c_mask = jnp.where(i >= CAP, base + i - CAP, -1) == r5
    f_row = base + 3 + lax.shift_right_logical(i, 2)
    g = lax.bitwise_and(i, 3)
    folds = [jnp.where(g == k, f_row, -1) == r5 for k in range(4)]
    return ones_where(x_mask), ones_where(c_mask), [ones_where(f) for f in folds]


def to_col(row, eye):
    return jnp.sum(jnp.where(eye, row, 0.0), axis=1, keepdims=True)


def kernel(
    cfg, tok_hbm, gain_hbm, routes_hbm, gates_hbm, win_ref, wout_ref, og_hbm,
    mixed_hbm, gg_hbm, tg_hbm, gin_hbm, gout_hbm,
    mixed_ref, gg_ref, tg_ref, gin_ref, gout_ref,
    tok_ref, gain_ref, routes_ref, gates_ref, og_ref,
    win, wout, send, recv, rsend, rrecv, rhs1, rhs2, std_ref,
    m1, m2, b1, b2, xs, cs, act, hg, gbuf, xbuf, sbuf, rbuf,
    in_sem, out_sem, w_sem, send_sem, recv_sem, rsend_sem, rrecv_sem, xs_sem, xr_sem, ss_sem, sr_sem,
):
    nz, ny, nch = cfg
    n_exp = NX * nz
    oc = n_exp // nch
    rows8, rows5 = oc * 8, oc * CAP
    frames, dim = tok_ref.shape
    ngrp = dim // LANES
    hid = win.shape[0]
    share = hid // (ny * CORES)
    half = ny // 2

    d = lax.axis_index("dp")
    e = lax.axis_index("expert")
    y, c = lax.div(d, CORES), lax.rem(d, CORES)
    x, z = lax.div(e, nz), lax.rem(e, nz)
    up = lax.rem(y + 1, ny) * CORES + c
    down = lax.rem(y + ny - 1, ny) * CORES + c
    mate = y * CORES + (1 - c)

    def column(p):
        odd = lax.rem(p, 2)
        return odd * lax.div(nz - 1 - p, 2) + (1 - odd) * lax.rem(nz // 2 + lax.div(p, 2), nz)

    to_x = [lax.rem(x + NX - 1 - xp, NX) * nz for xp in range(NX)]
    from_x = [lax.rem(x + 1 + xp, NX) * nz for xp in range(NX)]

    def to_z(p):
        return lax.rem(z + column(p), nz)

    def from_z(p):
        return lax.rem(z + nz - column(p), nz)

    def each_peer(first, last, act):
        def columns(p, carry):
            for xp in range(NX):
                act(p, xp)
            return carry

        lax.fori_loop(first, jnp.minimum(last, nz - 1), columns, 0)

        def rest():
            for xp in range(NX - 1):
                act(nz - 1, xp)

        if isinstance(last, int):
            rest()
        else:
            pl.when(last == nz)(rest)

    in_copies = [
        pltpu.make_async_copy(src, dst, in_sem.at[i])
        for i, (src, dst) in enumerate(
            (
                (routes_hbm, routes_ref),
                (gates_hbm, gates_ref),
                (tok_hbm, tok_ref),
                (gain_hbm, gain_ref),
                (og_hbm, og_ref),
            )
        )
    ]
    for copy in in_copies:
        copy.start()

    barrier = pltpu.get_barrier_semaphore()

    def greet(p, xp):
        pl.semaphore_signal(
            barrier, inc=1, device_id=(d, to_x[xp] + to_z(p)), device_id_type=MESH
        )

    each_peer(0, nz, greet)
    for other in (up, down, mate):
        pl.semaphore_signal(barrier, inc=1, device_id=(other, e), device_id_type=MESH)

    w_copies = [
        pltpu.make_async_copy(win_ref.at[0], win, w_sem.at[0]),
        pltpu.make_async_copy(wout_ref.at[0], wout, w_sem.at[1]),
    ]
    for copy in w_copies:
        copy.start()

    for copy in in_copies:
        copy.wait()
    values = tok_ref[...].astype(F32)
    centered = values - jnp.mean(values, axis=1, keepdims=True)
    inv_std = lax.rsqrt(jnp.mean(centered * centered, axis=1, keepdims=True) + EPS)
    standard = centered * inv_std
    std_ref[...] = standard
    gain = gain_ref[...]
    rhs1[0:frames, :] = (standard * gain).astype(BF)

    f_row = lax.broadcasted_iota(jnp.int32, (frames, frames), 0)
    f_col = lax.broadcasted_iota(jnp.int32, (frames, frames), 1)
    eye = f_row == f_col
    og = og_ref[...].astype(F32)
    gates = [to_col(gates_ref[k : k + 1, :], eye) for k in range(2)]
    for k in range(2):
        scaled = (gates[k] * og).astype(BF)
        rhs1[frames * (k + 1) : frames * (k + 2), :] = scaled
        for g in range(ngrp):
            at = (k * ngrp + g) * frames
            rhs2[at : at + frames, :] = scaled[:, g * LANES : (g + 1) * LANES]

    rels, hots = [], []
    e_iota = lax.broadcasted_iota(jnp.int32, (n_exp, frames), 0)
    for k in range(2):
        r = routes_ref[k : k + 1, :]
        dx = lax.bitwise_and(lax.shift_right_logical(r, nz.bit_length() - 1) - x, NX - 1)
        dz = lax.bitwise_and(r - z, nz - 1)
        p = jnp.where(dz < nz // 2, nz - 1 - 2 * dz, 2 * dz - nz)
        rel = p * NX + (NX - 1 - dx)
        rels.append(rel)
        hots.append(jnp.where(e_iota == rel, 1.0, 0.0))
    before = fdot((hots[0] + hots[1]).astype(BF), ones_where(f_row < f_col))
    dest_a, dest_b, dest_f = [], [], []
    for k in range(2):
        slot = jnp.sum(hots[k] * before, axis=0, keepdims=True)
        base = rels[k].astype(F32) * 8.0
        dest_a.append(base + slot)
        dest_b.append(jnp.where(slot < 3.0, base + 5.0 + slot, -1.0))
        dest_f.append(jnp.where(slot >= 3.0, base + (slot - 3.0) * 4.0, -100.0))

    pl.semaphore_wait(barrier, n_exp + 2)

    def dispatch(q, p, xp):
        o = p * NX + xp
        pltpu.make_async_remote_copy(
            src_ref=send.at[o], dst_ref=recv.at[o], send_sem=send_sem, recv_sem=recv_sem.at[q],
            device_id=(d, to_x[xp] + to_z(p)), device_id_type=MESH,
        ).start()

    def give_back(q, p, xp):
        o = p * NX + xp
        pltpu.make_async_remote_copy(
            src_ref=rsend.at[o], dst_ref=rrecv.at[o], send_sem=rsend_sem, recv_sem=rrecv_sem.at[q],
            device_id=(d, from_x[xp] + from_z(p)), device_id_type=MESH,
        ).start()

    grp = nz // nch
    own = n_exp - 1

    def send_chunk(q, carry):
        rid = (lax.broadcasted_iota(jnp.int32, (rows8, frames), 0) + q * rows8).astype(F32)
        a = ones_where((rid == dest_a[0]) | (rid == dest_a[1]))
        lhs1 = jnp.concatenate([a] + [ones_where(rid == dest_b[k]) for k in range(2)], axis=1)
        lhs2 = jnp.concatenate(
            [ones_where(rid == dest_f[k] + float(g)) for k in range(2) for g in range(ngrp)], axis=1
        )
        first = q * oc
        send[pl.ds(first, oc), :, 0:dim] = fdot(lhs1, rhs1[...]).reshape(oc, 8, dim).astype(BF)
        send[pl.ds(first, oc), :, dim : dim + LANES] = (
            fdot(lhs2, rhs2[...]).reshape(oc, 8, LANES).astype(BF)
        )

        each_peer(q * grp, q * grp + grp, functools.partial(dispatch, q))
        return carry

    lax.fori_loop(0, nch, send_chunk, 0)
    own_copy = pltpu.make_async_copy(send.at[own], recv.at[own], recv_sem.at[nch - 1])
    own_copy.start()

    xm, cm, fm = route_rows((rows5, rows8), 1)
    m1[0:rows5, :] = xm
    m1[rows5 : 2 * rows5, :] = cm
    for g in range(ngrp):
        m2[g * rows5 : (g + 1) * rows5, :] = fm[g]
    xt, ct, ft = route_rows((rows8, rows5), 0)
    b1[...] = jnp.concatenate([xt, ct], axis=1)
    b2[...] = jnp.concatenate(ft, axis=1)

    for copy in w_copies:
        copy.wait()

    n_blk = 4
    blk = hid // n_blk
    nt = (((1,), (1,)), ((), ()))

    def return_chunk(q):
        each_peer(q * grp, q * grp + grp, functools.partial(give_back, q))

    def expert_chunk(q, carry):
        first = q * oc
        row = pl.multiple_of(q * rows5, rows5)
        pltpu.make_async_copy(
            recv.at[pl.ds(first, oc)], recv.at[pl.ds(first, oc)], recv_sem.at[q]
        ).wait()
        if DELAY:
            pl.when(q >= DELAY)(lambda: return_chunk(q - DELAY))
        msg = recv[pl.ds(first, oc)].astype(F32).reshape(rows8, dim + LANES).astype(BF)
        both = fdot(m1[...], msg[:, 0:dim])
        folded = fdot(m2[...], msg[:, dim : dim + LANES])
        x_in = both[0:rows5].astype(BF)
        fold_cat = jnp.concatenate(
            [folded[g * rows5 : (g + 1) * rows5] for g in range(ngrp)], axis=1
        )
        cot = (both[rows5 : 2 * rows5] + fold_cat).astype(BF)
        xs[pl.ds(row, rows5), :] = x_in
        cs[pl.ds(row, rows5), :] = cot
        out = jnp.zeros((rows5, dim), F32)
        ingrad = jnp.zeros((rows5, dim), F32)
        for b in range(n_blk):
            at = slice(b * blk, (b + 1) * blk)
            pre = lax.dot_general(x_in, win[at, :], nt, preferred_element_type=F32)
            back = lax.dot_general(cot, wout[at, :], nt, preferred_element_type=F32)
            sg = 0.5 * jnp.tanh(0.5 * pre) + 0.5
            act_b = (pre * sg).astype(BF)
            hg_b = (back * (sg * (1.0 + pre * (1.0 - sg)))).astype(BF)
            act[pl.ds(row, rows5), at] = act_b
            hg[pl.ds(row, rows5), at] = hg_b
            out = out + fdot(act_b, wout[at, :])
            ingrad = ingrad + fdot(hg_b, win[at, :])
        out_h, in_h = out.astype(BF), ingrad.astype(BF)
        rmain = fdot(b1[...], jnp.concatenate([out_h, in_h], axis=0))
        stack = jnp.concatenate(
            [in_h[:, g * LANES : (g + 1) * LANES] for g in range(ngrp)], axis=0
        )
        rfold = fdot(b2[...], stack)
        rsend[pl.ds(first, oc), :, 0:dim] = rmain.reshape(oc, 8, dim).astype(BF)
        rsend[pl.ds(first, oc), :, dim : dim + LANES] = rfold.reshape(oc, 8, LANES).astype(BF)

        return carry

    lax.fori_loop(0, nch, expert_chunk, 0)

    tn = (((0,), (0,)), ((), ()))

    def exchange(j):
        return pltpu.make_async_remote_copy(
            src_ref=gbuf.at[j, :, pl.ds((1 - c) * share, share), :], dst_ref=xbuf.at[j],
            send_sem=xs_sem.at[j], recv_sem=xr_sem.at[j], device_id=(mate, e), device_id_type=MESH,
        )

    def grads(j):
        shift = half - (j + 1) // 2 if j % 2 else (half + j // 2) % ny
        at = pl.multiple_of(lax.rem(y + shift, ny) * (CORES * share), CORES * share)
        cols = pl.ds(at, CORES * share)
        gbuf[j, 0] = lax.dot_general(hg[:, cols], xs[...], tn, preferred_element_type=F32).astype(BF)
        gbuf[j, 1] = lax.dot_general(act[:, cols], cs[...], tn, preferred_element_type=F32).astype(BF)
        exchange(j).start()

    def term(j, part):
        mine = gbuf[j, part, pl.ds(pl.multiple_of(c * share, share), share), :].astype(F32)
        return mine + xbuf[j, part].astype(F32)

    def hop(way, step, part):
        return pltpu.make_async_remote_copy(
            src_ref=sbuf.at[way, step, part], dst_ref=rbuf.at[way, step, part],
            send_sem=ss_sem.at[way, step, part], recv_sem=sr_sem.at[way, step, part],
            device_id=((up, down)[way], e), device_id_type=MESH,
        )

    def parts_of(way, step):
        return ((way,) if step == 0 else (1 - way, way))

    hops = []
    grads(0)
    if DELAY:
        lax.fori_loop(nch - DELAY, nch, lambda q, carry: (return_chunk(q), carry)[1], 0)
    own_back = pltpu.make_async_copy(rsend.at[own], rrecv.at[own], rrecv_sem.at[nch - 1])
    own_back.start()
    for step in range(half):
        js = (0,) if step == 0 else (2 * step - 1, 2 * step)
        ahead = [j for j in (2 * step, 2 * step + 1) if 0 < j < ny]
        for j in ahead:
            grads(j)
        for j in js:
            exchange(j).wait_recv()
        order = (0, 1) if step == 1 or step == 0 else (0, 1)
        for i in order:
            for way in range(2):
                parts = parts_of(way, step)
                if i >= len(parts):
                    continue
                part = parts[i]
                j = js[way] if step else 0
                total = term(j, part)
                if step and part in parts_of(way, step - 1):
                    hop(way, step - 1, part).wait_recv()
                    total = total + rbuf[way, step - 1, part].astype(F32)
                sbuf[way, step, part] = total.astype(BF)
                copy = hop(way, step, part)
                copy.start()
                hops.append(copy)

    lane_id = lax.broadcasted_iota(jnp.int32, (frames, n_exp * 8), 1).astype(F32)
    cols_a = [to_col(dest_a[k], eye) for k in range(2)]
    cols_b = [to_col(dest_b[k], eye) for k in range(2)]
    cols_f = [to_col(dest_f[k], eye) for k in range(2)]
    pick_a = [ones_where(lane_id == cols_a[k]) for k in range(2)]
    pick_b = ones_where((lane_id == cols_b[0]) | (lane_id == cols_b[1]))
    pick_f = [
        ones_where((lane_id == cols_f[0] + float(g)) | (lane_id == cols_f[1] + float(g)))
        for g in range(ngrp)
    ]
    outs = [
        pltpu.make_async_copy(src, dst, out_sem.at[i])
        for i, (src, dst) in enumerate(
            (
                (mixed_ref, mixed_hbm),
                (gg_ref, gg_hbm),
                (tg_ref, tg_hbm),
                (gin_ref, gin_hbm),
                (gout_ref, gout_hbm),
            )
        )
    ]

    last = half - 1
    exchange(ny - 1).wait_recv()
    for part, out_ref in ((0, gin_ref), (1, gout_ref)):
        total = term(ny - 1, part)
        for way in range(2):
            if part in parts_of(way, last):
                hop(way, last, part).wait_recv()
                total = total + rbuf[way, last, part].astype(F32)
        out_ref[0] = total
        outs[3 + part].start()

    y_rows = [jnp.zeros((frames, dim), F32) for k in range(2)]
    du = jnp.zeros((frames, dim), F32)
    for q in range(nch):
        pltpu.make_async_copy(
            rrecv.at[pl.ds(q * oc, oc)], rrecv.at[pl.ds(q * oc, oc)], rrecv_sem.at[q]
        ).wait()
        msg = rrecv[q * oc : (q + 1) * oc].astype(F32).reshape(rows8, dim + LANES).astype(BF)
        main, fold = msg[:, 0:dim], msg[:, dim : dim + LANES]
        at = slice(q * rows8, (q + 1) * rows8)
        y_rows = [y_rows[k] + fdot(pick_a[k][:, at], main) for k in range(2)]
        folded = [fdot(pick_f[g][:, at], fold) for g in range(ngrp)]
        du = du + fdot(pick_b[:, at], main) + jnp.concatenate(folded, axis=1)
    og = og_ref[...].astype(F32)
    mixed_ref[...] = (gates[0] * y_rows[0] + gates[1] * y_rows[1]).astype(BF)
    for k in range(2):
        dots = jnp.sum(og * y_rows[k], axis=1, keepdims=True)
        gg_ref[k : k + 1, :] = jnp.sum(jnp.where(eye, dots, 0.0), axis=0, keepdims=True)
    norm_grad = du * gain
    standard = std_ref[...]
    tg_ref[...] = (
        inv_std
        * (
            norm_grad
            - jnp.mean(norm_grad, axis=1, keepdims=True)
            - standard * jnp.mean(norm_grad * standard, axis=1, keepdims=True)
        )
    ).astype(BF)

    for i in range(3):
        outs[i].start()

    pltpu.make_async_copy(send.at[pl.ds(0, own)], send.at[pl.ds(0, own)], send_sem).wait()
    pltpu.make_async_copy(rsend.at[pl.ds(0, own)], rsend.at[pl.ds(0, own)], rsend_sem).wait()
    for j in range(ny):
        exchange(j).wait_send()
    for copy in hops:
        copy.wait_send()
    for copy in outs:
        copy.wait()


def store_kernel(*refs):
    n = (len(refs) - 1) // 2
    copies = [
        pltpu.make_async_copy(refs[i], refs[n + i], refs[2 * n].at[i]) for i in range(n)
    ]
    for copy in copies:
        copy.start()
    for copy in copies:
        copy.wait()


def store(*arrays):
    return pl.pallas_call(
        store_kernel,
        out_shape=tuple(jax.ShapeDtypeStruct(a.shape, a.dtype) for a in arrays),
        in_specs=[pl.BlockSpec(memory_space=pltpu.VMEM)] * len(arrays),
        out_specs=(pl.BlockSpec(memory_space=pltpu.HBM),) * len(arrays),
        scratch_shapes=[pltpu.SemaphoreType.DMA((len(arrays),))],
        compiler_params=pltpu.CompilerParams(vmem_limit_bytes=VMEM_BYTES),
    )(*arrays)


def local(nz, ny, nch, tokens, norm_gain, routes, gate_weights, weight_in, weight_out, out_grad):
    frames, dim = tokens.shape
    hid = weight_in.shape[1]
    n_exp = NX * nz
    oc = n_exp // nch
    share = hid // (ny * CORES)
    half = ny // 2
    ngrp = dim // LANES
    total = n_exp * CAP
    msgs = pltpu.VMEM((n_exp, 8, dim + LANES), BF)
    dma = pltpu.SemaphoreType.DMA
    hbm = pl.BlockSpec(memory_space=pltpu.HBM)
    mixed, gate_grad, token_grad, gin, gout = pl.pallas_call(
        functools.partial(kernel, (nz, ny, nch)),
        out_shape=(
            jax.ShapeDtypeStruct((frames, dim), BF),
            jax.ShapeDtypeStruct((2, frames), F32),
            jax.ShapeDtypeStruct((frames, dim), BF),
            jax.ShapeDtypeStruct((1, share, dim), F32),
            jax.ShapeDtypeStruct((1, share, dim), F32),
        ),
        in_specs=[hbm] * 7,
        out_specs=(hbm,) * 5,
        scratch_shapes=[
            pltpu.VMEM((frames, dim), BF),
            pltpu.VMEM((2, frames), F32),
            pltpu.VMEM((frames, dim), BF),
            pltpu.VMEM((1, share, dim), F32),
            pltpu.VMEM((1, share, dim), F32),
            pltpu.VMEM((frames, dim), BF),
            pltpu.VMEM((1, dim), F32),
            pltpu.VMEM((2, frames), jnp.int32),
            pltpu.VMEM((2, frames), F32),
            pltpu.VMEM((frames, dim), BF),
            pltpu.VMEM((hid, dim), BF),
            pltpu.VMEM((hid, dim), BF),
            msgs, msgs, msgs, msgs,
            pltpu.VMEM((3 * frames, dim), BF),
            pltpu.VMEM((2 * ngrp * frames, LANES), BF),
            pltpu.VMEM((frames, dim), F32),
            pltpu.VMEM((2 * oc * CAP, oc * 8), BF),
            pltpu.VMEM((ngrp * oc * CAP, oc * 8), BF),
            pltpu.VMEM((oc * 8, 2 * oc * CAP), BF),
            pltpu.VMEM((oc * 8, ngrp * oc * CAP), BF),
            pltpu.VMEM((total, dim), BF),
            pltpu.VMEM((total, dim), BF),
            pltpu.VMEM((total, hid), BF),
            pltpu.VMEM((total, hid), BF),
            pltpu.VMEM((ny, 2, CORES * share, dim), BF),
            pltpu.VMEM((ny, 2, share, dim), BF),
            pltpu.VMEM((2, half, 2, share, dim), BF),
            pltpu.VMEM((2, half, 2, share, dim), BF),
            dma((5,)), dma((5,)), dma((2,)), dma, dma((nch,)), dma, dma((nch,)),
            dma((ny,)), dma((ny,)), dma((2, half, 2)), dma((2, half, 2)),
        ],
        compiler_params=pltpu.CompilerParams(
            collective_id=0, has_side_effects=True, vmem_limit_bytes=VMEM_BYTES
        ),
    )(
        tokens, norm_gain.reshape(1, dim), routes.T, gate_weights.T, weight_in, weight_out, out_grad
    )
    mixed, gate_grad, token_grad, gin, gout = store(mixed, gate_grad, token_grad, gin, gout)
    return mixed, gate_grad.T, token_grad, gin, gout


def solution(mesh):
    nz = mesh.shape["expert"] // NX
    ny = mesh.shape["dp"] // CORES
    frames = P(("dp", "expert"), None)
    weights = P("expert", None, None)
    return jax.shard_map(
        functools.partial(local, nz, ny, 4),
        mesh=mesh,
        in_specs=(frames, P(), frames, frames, weights, weights, frames),
        out_specs=(frames, frames, frames, P("expert", "dp", None), P("expert", "dp", None)),
        check_vma=False,
    )
```
